256 devices in a mesh: ctx: 64 (over y, z, x_lo), dp: 4 (over x_hi, core).
Axes of the slice: x: 4 (x_hi: 2, x_lo: 2; x = x_hi * 2 + x_lo), y: 4, z: 8, core: 2. Of those that a mesh axis runs over, the one named last changes fastest.
Arguments:
- queries: bfloat16 [65536, 512], P(('dp', 'ctx')), parts along dimension 0, may hold values from -6 to 6
- key_head: bfloat16 [65536, 128], P(('dp', 'ctx')), parts along dimension 0, may hold values from -6 to 6
- value_head: bfloat16 [65536, 128], P(('dp', 'ctx')), parts along dimension 0, may hold values from -6 to 6
- attn_out: bfloat16 [65536, 512], P(('dp', 'ctx')), parts along dimension 0, may hold values from -3 to 3
- out_grads: bfloat16 [65536, 512], P(('dp', 'ctx')), parts along dimension 0, may hold values from -24 to 24
- log_norms: float32 [4, 65536], P(None, ('dp', 'ctx')), parts along dimension 1, may hold values from -1 to 14
- pairing: int32 [256], P('dp'), parts along dimension 0, may hold values from 0 to 63, as said below
Outputs:
- query_grad: float32 [65536, 512], P(('dp', 'ctx')), parts along dimension 0
- key_grad: float32 [65536, 128], P(('dp', 'ctx')), parts along dimension 0
- value_grad: float32 [65536, 128], P(('dp', 'ctx')), parts along dimension 0
The draws below stay inside these ranges and needn't reach their ends.
There are 4 independent parts, one for each index of `dp`. The reference program is written for one: setup_inputs(seed, part) draws one part's arguments, and reference() takes and returns one part's arrays. A program takes and returns all parts, laid end to end along the dimension named above; each array names one. Nothing has to cross between parts.
Inputs may be any that keep to these rules, and one draw needn't show every extreme that they name: pairing is a permutation of 0 to 63.
All inputs are finite; a program needn't handle non-finite values.
Results may differ from the reference program's by a relative error of at most 0.0029.
Values may be sent and summed in bfloat16 or wider, within the bound.
No kernel may reach another device: no remote copies, remote signals or barrier semaphores. Data moves between devices by JAX's collectives and lax.ppermute only.
A program may use at most 128 MiB of HBM per device.

```python
import math
import jax
import jax.numpy as jnp
from jax import lax

HEAD = 128
HEADS = 4
S_DEV = 256
HALF = 128
SHARDS = 64
TOKENS = 16384


def shared_pairing(key):
    return jax.random.permutation(key, SHARDS).astype(jnp.int32)


def draw_pairing(key, part):
    return shared_pairing(key)


def draw_log_norms(key, part):
    ranks = shared_pairing(key)
    key = jax.random.fold_in(key, 2)
    row_index = jnp.arange(TOKENS, dtype=jnp.int32)
    shard_of = row_index // S_DEV
    is_upper = row_index % S_DEV // HALF
    own_block = ranks[shard_of]
    block_of = jnp.where(is_upper == 0, own_block, 2 * SHARDS - 1 - own_block)
    positions = block_of * HALF + row_index % HALF
    base_level = jnp.log((positions + 1).astype(jnp.float32)) + 0.5
    spread = jnp.clip(0.4 * jax.random.normal(key, (HEADS, TOKENS), jnp.float32), -1.0, 1.0)
    return base_level[None, :] + spread


def levels(key, extent, shards, smallest, largest):
    level = 1.0
    for axis_at, blocks in shards:
        draws = jax.random.uniform(jax.random.fold_in(jax.random.fold_in(key, 6), axis_at), (blocks,), jnp.float32, smallest / len(shards), largest / len(shards))
        level = level * jnp.repeat(jnp.exp(draws), extent[axis_at] // blocks).reshape((-1,) + (1,) * (len(extent) - 1 - axis_at))
    return level


def scatter_about(own_key, dims, scale, most, shards=(), kind=jnp.bfloat16):
    factor_of = levels(own_key, dims, shards, -0.22, 0.18) if shards else 1.0
    values = jax.random.normal(own_key, dims, jnp.float32) * scale * factor_of
    return jnp.minimum(jnp.maximum(values, -most), most).astype(kind)


def setup_inputs(seed: int = 0, part: int = 0) -> dict:
    keys = jax.random.split(jax.random.key(seed), 8)
    part_keys = jax.random.split(jax.random.fold_in(keys[7], part), 8)
    return {
        "queries": scatter_about(part_keys[0], (TOKENS, HEADS * HEAD), 1.0, 6.0, ((0, 64),)),
        "key_head": scatter_about(part_keys[1], (TOKENS, HEAD), 1.0, 6.0, ((0, 64),)),
        "value_head": scatter_about(part_keys[2], (TOKENS, HEAD), 1.0, 6.0, ((0, 64),)),
        "attn_out": scatter_about(part_keys[3], (TOKENS, HEADS * HEAD), 0.5, 3.0, ((0, 64),)),
        "out_grads": scatter_about(part_keys[4], (TOKENS, HEADS * HEAD), 4.0, 24.0, ((0, 64),)),
        "log_norms": draw_log_norms(jax.random.fold_in(jax.random.fold_in(keys[7], part), 71), part),
        "pairing": draw_pairing(jax.random.fold_in(jax.random.fold_in(keys[7], part), 71), part),
    }


def reference(queries, key_head, value_head, attn_out, out_grads, log_norms, pairing):
    score_scale = 1.0 / math.sqrt(HEAD)
    row_index = jnp.arange(TOKENS, dtype=jnp.int32)
    shard_of = row_index // S_DEV
    is_upper = row_index % S_DEV // HALF
    within_block = row_index % HALF
    own_block = pairing[shard_of].astype(jnp.int32)
    block_of = jnp.where(is_upper == 0, own_block, 2 * SHARDS - 1 - own_block)
    positions = (block_of * HALF + within_block).astype(jnp.int32)
    keys_wide = key_head.astype(jnp.float32)
    values_wide = value_head.astype(jnp.float32)
    deltas = lax.optimization_barrier(jnp.sum((attn_out.astype(jnp.float32) * out_grads.astype(jnp.float32)).reshape(TOKENS, HEADS, HEAD), axis=2))
    query_blocks = queries.astype(jnp.float32).reshape(SHARDS, S_DEV, HEADS, HEAD)
    grad_blocks = out_grads.astype(jnp.float32).reshape(SHARDS, S_DEV, HEADS, HEAD)
    norm_blocks = log_norms.reshape(HEADS, SHARDS, S_DEV).transpose(1, 0, 2)
    delta_blocks = deltas.reshape(SHARDS, S_DEV, HEADS).transpose(0, 2, 1)
    position_blocks = positions.reshape(SHARDS, S_DEV)

    def block_step(carry, inputs):
        key_total, value_total = carry
        query_rows, grad_rows, norm_rows, delta_rows, position_rows = inputs
        scores = jnp.einsum('qhd,kd->hqk', query_rows, keys_wide, precision=lax.Precision.HIGHEST) * score_scale
        visible = position_rows[:, None] >= positions[None, :]
        probs = jnp.where(visible[None], jnp.exp(scores - norm_rows[:, :, None]), 0.0)
        dprobs = jnp.einsum('qhd,kd->hqk', grad_rows, values_wide, precision=lax.Precision.HIGHEST)
        dscores = (probs * (dprobs - delta_rows[:, :, None]) * score_scale).astype(jnp.bfloat16)
        dscores = lax.optimization_barrier(dscores).astype(jnp.float32)
        probs_low = lax.optimization_barrier(probs.astype(jnp.bfloat16)).astype(jnp.float32)
        value_total = value_total + jnp.einsum('hqk,qhd->kd', probs_low, grad_rows, precision=lax.Precision.HIGHEST)
        key_total = key_total + jnp.einsum('hqk,qhd->kd', dscores, query_rows, precision=lax.Precision.HIGHEST)
        query_part = jnp.einsum('hqk,kd->qhd', dscores, keys_wide, precision=lax.Precision.HIGHEST)
        return ((key_total, value_total), query_part.reshape(S_DEV, HEADS * HEAD))
    start_carry = (jnp.zeros((TOKENS, HEAD), jnp.float32), jnp.zeros((TOKENS, HEAD), jnp.float32))
    (key_grad, value_grad), query_parts = lax.scan(block_step, start_carry, (query_blocks, grad_blocks, norm_blocks, delta_blocks, position_blocks))
    return (query_parts.reshape(TOKENS, HEADS * HEAD), key_grad, value_grad)
```

```python
import math

import jax
import jax.numpy as jnp
from jax import lax
from jax.experimental import pallas as pl
from jax.experimental.pallas import tpu as pltpu
from jax.sharding import PartitionSpec as P

F32 = jnp.float32
BF16 = jnp.bfloat16
HEAD = 128
HEADS = 4
HALF = 128
ROWS = HEADS * HALF
NY, NZ, NX = 4, 8, 2
SCALE = 1.0 / math.sqrt(HEAD)
LOG2E = math.log2(math.e)
NT = (((1,), (1,)), ((), ()))
TN = (((0,), (0,)), ((), ()))
CHUNK = 4


def dot(a, b, dims):
    return lax.dot_general(a, b, dims, preferred_element_type=F32)


def attention_kernel(n_q, n_k, *refs):
    rq, rk = refs[:2]
    q_refs = refs[2 : 2 + n_q]
    g_refs = refs[2 + n_q : 2 + 2 * n_q]
    st_refs = refs[2 + 2 * n_q : 2 + 3 * n_q]
    at = 2 + 3 * n_q
    kv_refs = refs[at : at + n_k]
    own_dq, far_dq, own_dkv, far_dkv = refs[at + n_k : at + n_k + 4]
    qs, gs, ns, ds, ks, vs, dks, dvs, acc = refs[at + n_k + 4 :]
    for d in range(n_q):
        for half in range(2):
            i = 2 * d + half
            rows = slice(half * HALF, (half + 1) * HALF)
            for h in range(HEADS):
                cols = slice(h * HEAD, (h + 1) * HEAD)
                qs[i, cols, :] = q_refs[d][rows, cols]
                gs[i, cols, :] = g_refs[d][rows, cols]
                ns[i, :, cols] = st_refs[d][h : h + 1, rows] * LOG2E
                ds[i, :, cols] = st_refs[d][HEADS + h : HEADS + h + 1, rows]
    for e in range(n_k):
        for half in range(2):
            rows = slice(half * HALF, (half + 1) * HALF)
            ks[half, e * HALF : (e + 1) * HALF, :] = kv_refs[e][rows, :HEAD]
            vs[half, e * HALF : (e + 1) * HALF, :] = kv_refs[e][rows, HEAD:]
    acc[...] = jnp.zeros_like(acc)

    def tile(i, k, v, keep=None):
        q, g = qs[i], gs[i]
        scores = dot(k, q, NT)
        probs = jnp.exp2(scores * (SCALE * LOG2E) - ns[i])
        if keep is not None:
            probs = jnp.where(keep, probs, 0.0)
        dprobs = dot(v, g, NT)
        dscores = (probs * (dprobs - ds[i]) * SCALE).astype(BF16)
        probs_low = probs.astype(BF16)
        dv = jnp.dot(probs_low, g, preferred_element_type=F32)
        dk = jnp.dot(dscores, q, preferred_element_type=F32)
        acc[i] += dot(k, dscores, TN)
        return dk, dv

    def first(c, carry):
        keys = pl.ds(pl.multiple_of(c * (CHUNK * HALF), CHUNK * HALF), CHUNK * HALF)
        k, v = ks[0, keys, :], vs[0, keys, :]
        dk = dv = 0.0
        for d in range(n_q):
            x, y = tile(2 * d + 1, k, v)
            dk, dv = dk + x, dv + y
        dks[0, keys, :] = dk
        dvs[0, keys, :] = dv
        dks[1, keys, :] = jnp.zeros_like(dk)
        dvs[1, keys, :] = jnp.zeros_like(dv)
        return carry

    lax.fori_loop(0, n_k // CHUNK, first, 0)

    def second(e, d):
        half = jnp.where(rk[e] < rq[d], 0, 1)
        keys = pl.ds(pl.multiple_of(e * HALF, HALF), HALF)
        x, y = tile(2 * d + half, ks[half, keys, :], vs[half, keys, :])
        dks[half, keys, :] += x
        dvs[half, keys, :] += y

    def second_all(e, carry):
        for d in range(n_q):
            second(e, d)
        return carry

    lax.fori_loop(1, n_k, second_all, 0)
    for d in range(1, n_q):
        second(0, d)
    key_at = lax.broadcasted_iota(jnp.int32, (HALF, ROWS), 0)
    row_at = lax.broadcasted_iota(jnp.int32, (HALF, ROWS), 1) & (HALF - 1)
    keep = row_at >= key_at
    for half in range(2):
        x, y = tile(half, ks[half, :HALF, :], vs[half, :HALF, :], keep)
        dks[half, :HALF, :] += x
        dvs[half, :HALF, :] += y
    for d in range(n_q):
        for half in range(2):
            rows = slice(half * HALF, (half + 1) * HALF)
            for h in range(HEADS):
                cols = slice(h * HEAD, (h + 1) * HEAD)
                block = acc[2 * d + half, :, cols].T
                if d == 0:
                    own_dq[rows, cols] = block
                else:
                    far_dq[d - 1, rows, cols] = block.astype(BF16)
    for e in range(n_k):
        keys = slice(e * HALF, (e + 1) * HALF)
        for half in range(2):
            rows = slice(half * HALF, (half + 1) * HALF)
            if e % 2 == 0:
                own_dkv[e // 2, rows, :HEAD] = dks[half, keys, :]
                own_dkv[e // 2, rows, HEAD:] = dvs[half, keys, :]
            else:
                far_dkv[e // 2, rows, :HEAD] = dks[half, keys, :].astype(BF16)
                far_dkv[e // 2, rows, HEAD:] = dvs[half, keys, :].astype(BF16)


def attention(rq, rk, queries, grads, stats, kvs):
    n_q, n_k = len(queries), len(kvs)
    pairs = n_q * n_k
    smem = pl.BlockSpec(memory_space=pltpu.SMEM)
    vmem = pl.BlockSpec(memory_space=pltpu.VMEM)

    def kernel(*refs):
        attention_kernel(n_q, n_k, *refs)

    return pl.pallas_call(
        kernel,
        out_shape=(
            jax.ShapeDtypeStruct((2 * HALF, ROWS), F32),
            jax.ShapeDtypeStruct((n_q - 1, 2 * HALF, ROWS), BF16),
            jax.ShapeDtypeStruct((n_k // 2, 2 * HALF, 2 * HEAD), F32),
            jax.ShapeDtypeStruct((n_k // 2, 2 * HALF, 2 * HEAD), BF16),
        ),
        in_specs=[smem, smem] + [vmem] * (3 * n_q + n_k),
        out_specs=(vmem,) * 4,
        scratch_shapes=[
            pltpu.VMEM((2 * n_q, ROWS, HEAD), BF16),
            pltpu.VMEM((2 * n_q, ROWS, HEAD), BF16),
            pltpu.VMEM((2 * n_q, 1, ROWS), F32),
            pltpu.VMEM((2 * n_q, 1, ROWS), F32),
            pltpu.VMEM((2, n_k * HALF, HEAD), BF16),
            pltpu.VMEM((2, n_k * HALF, HEAD), BF16),
            pltpu.VMEM((2, n_k * HALF, HEAD), F32),
            pltpu.VMEM((2, n_k * HALF, HEAD), F32),
            pltpu.VMEM((2 * n_q, HEAD, ROWS), F32),
        ],
        compiler_params=pltpu.CompilerParams(vmem_limit_bytes=44 * 1024 * 1024),
        cost_estimate=pl.CostEstimate(
            flops=pairs * 2 * 5 * 2 * HALF * HALF * ROWS,
            bytes_accessed=8 * 1024 * 1024,
            transcendentals=pairs * 2 * HALF * ROWS,
        ),
    )(rq, rk, *queries, *grads, *stats, *kvs)


def index_of(y, z, x):
    return (y * NZ + z) * NX + x


def shift(dy, dz, flip):
    return [
        (index_of((y + dy) % NY, (z + dz) % NZ, x ^ flip), index_of(y, z, x))
        for y in range(NY)
        for z in range(NZ)
        for x in range(NX)
    ]


def fetch(array, dy=0, dz=0, flip=0):
    return lax.ppermute(array, "ctx", shift(dy % NY, dz % NZ, flip))


def body(queries, key_head, value_head, attn_out, out_grads, log_norms, pairing):
    me = lax.axis_index("ctx")
    x, z, y = me % NX, (me // NX) % NZ, me // (NX * NZ)
    shards = jnp.arange(NY * NZ * NX, dtype=jnp.int32)

    def rank_of(index):
        return jnp.sum(jnp.where(index[:, None] == shards, pairing, 0), axis=-1)

    q_at = index_of((y + jnp.arange(NY)) % NY, z, x)
    k_slot = jnp.arange(NZ * NX)
    k_at = index_of(y, (z + k_slot // NX) % NZ, x ^ (k_slot % NX))
    rq, rk = rank_of(q_at), rank_of(k_at)

    kv = jnp.concatenate([key_head, value_head], axis=1)
    near = [kv] + [fetch(kv, dz=r) for r in range(1, NZ)]
    kvs = []
    for block in near:
        kvs += [block, fetch(block, flip=1)]
    deltas = jnp.sum(
        (attn_out.astype(F32) * out_grads.astype(F32)).reshape(2 * HALF, HEADS, HEAD), axis=2
    )
    stat = jnp.concatenate([log_norms, deltas.T], axis=0)
    qs = [queries] + [fetch(queries, dy=r) for r in range(1, NY)]
    gs = [out_grads] + [fetch(out_grads, dy=r) for r in range(1, NY)]
    stats = [stat] + [fetch(stat, dy=r) for r in range(1, NY)]

    own_dq, far_dq, own_dkv, far_dkv = attention(rq, rk, qs, gs, stats, kvs)

    other = fetch(far_dkv, flip=1)
    dq = own_dq
    for r in range(1, NY):
        dq = dq + fetch(far_dq[r - 1], dy=-r).astype(F32)
    mixed = own_dkv + other.astype(F32)
    dkv = mixed[0]
    for r in range(1, NZ):
        dkv = dkv + fetch(mixed[r].astype(BF16), dz=-r).astype(F32)
    return dq, dkv[:, :HEAD], dkv[:, HEAD:]


def solution(mesh):
    rows = P(("dp", "ctx"), None)
    in_specs = (rows,) * 5 + (P(None, ("dp", "ctx")), P("dp"))
    return jax.shard_map(
        body, mesh=mesh, in_specs=in_specs, out_specs=(rows,) * 3, check_vma=False
    )
```

```python
import math

import jax
import jax.numpy as jnp
from jax import lax
from jax.experimental import pallas as pl
from jax.experimental.pallas import tpu as pltpu
from jax.sharding import PartitionSpec as P

F32 = jnp.float32
BF16 = jnp.bfloat16
HEAD = 128
HEADS = 4
HALF = 128
ROWS = HEADS * HALF
NY, NZ, NX = 4, 8, 2
SCALE = 1.0 / math.sqrt(HEAD)
LOG2E = math.log2(math.e)
NT = (((1,), (1,)), ((), ()))
TN = (((0,), (0,)), ((), ()))
PACK = 2 * 2 * ROWS
STATS = 48
OPEN = (0, 1, 2, 3, 6, 7)
STAGES = ((4, 5), (3, 6), (2, 7), (1, 0))


def dot(a, b, dims):
    return lax.dot_general(a, b, dims, preferred_element_type=F32)


def pack_kernel(q_in, g_in, o_in, n_in, k_in, v_in, pack, kv, q_ref, g_ref, o_ref, n_ref, k_ref, v_ref, sems):
    pairs = [(k_in, k_ref), (v_in, v_ref), (q_in, q_ref), (g_in, g_ref), (o_in, o_ref), (n_in, n_ref)]
    copies = [pltpu.make_async_copy(s, t, sems.at[i]) for i, (s, t) in enumerate(pairs)]
    for copy in copies:
        copy.start()
    for copy in copies:
        copy.wait()
    for half in range(2):
        rows = slice(half * HALF, (half + 1) * HALF)
        kv[half, 0] = k_ref[rows, :]
        kv[half, 1] = v_ref[rows, :]
    terms = []
    for half in range(2):
        rows = slice(half * HALF, (half + 1) * HALF)
        deltas = []
        for h in range(HEADS):
            cols = slice(h * HEAD, (h + 1) * HEAD)
            q, g = q_ref[rows, cols], g_ref[rows, cols]
            at = half * 2 * ROWS + h * HALF
            pack[at : at + HALF, :] = q
            pack[at + ROWS : at + ROWS + HALF, :] = g
            product = o_ref[rows, cols].astype(F32) * g.astype(F32)
            deltas.append(jnp.sum(product.T, axis=0, keepdims=True))
        rest = jnp.concatenate([n_ref[:, rows] * LOG2E] + deltas, axis=0)
        for _ in range(3):
            term = rest.astype(BF16).astype(F32)
            rest = rest - term
            terms.append(term)
    pack[PACK:, :] = jnp.concatenate(terms, axis=0).astype(BF16)


def pack_inputs(queries, out_grads, attn_out, log_norms, key_head, value_head):
    vmem = pl.BlockSpec(memory_space=pltpu.VMEM)
    arrays = (queries, out_grads, attn_out, log_norms, key_head, value_head)
    return pl.pallas_call(
        pack_kernel,
        out_shape=(
            jax.ShapeDtypeStruct((PACK + STATS, HEAD), BF16),
            jax.ShapeDtypeStruct((2, 2, HALF, HEAD), BF16),
        ),
        in_specs=[pl.BlockSpec(memory_space=pl.ANY)] * 6,
        out_specs=(vmem,) * 2,
        scratch_shapes=[pltpu.VMEM(array.shape, array.dtype) for array in arrays]
        + [pltpu.SemaphoreType.DMA((6,))],
        compiler_params=pltpu.CompilerParams(vmem_limit_bytes=56 * 1024 * 1024),
    )(*arrays)


def stage_kernel(near, is_first, is_last, *refs):
    m = len(near)
    n_k = NX * m
    me_ref, pairing = refs[:2]
    packs = refs[2 : 2 + NY]
    blocks = refs[2 + NY : 2 + NY + m]
    at = 2 + NY + m
    acc_in = None
    if not is_first:
        acc_in = refs[at]
        at += 1
    dkv_refs = refs[at : at + m]
    at += m
    if is_last:
        dq_refs = refs[at : at + NY]
        at += NY
        acc = refs[at]
    else:
        acc = refs[at]
    at += 1
    ns, ds, ks, vs, dks, dvs, rk = refs[at:]

    me = me_ref[0]
    x, z, y = me & 1, (me >> 1) & (NZ - 1), me >> 4
    rq = [pairing[index_of((y + d) & (NY - 1), z, x)] for d in range(NY)]
    for i, r in enumerate(near):
        for s in range(NX):
            rk[NX * i + s] = pairing[index_of(y, (z + r) & (NZ - 1), x ^ s)]
            e = NX * i + s
            for half in range(2):
                ks[half, e * HALF : (e + 1) * HALF, :] = blocks[i][s, half, 0]
                vs[half, e * HALF : (e + 1) * HALF, :] = blocks[i][s, half, 1]
    for d in range(NY):
        terms = packs[d][PACK:, :].astype(F32)
        for half in range(2):
            t = terms[24 * half : 24 * half + 24]
            stat = (t[0:8] + t[8:16]) + t[16:24]
            for h in range(HEADS):
                cols = slice(h * HALF, (h + 1) * HALF)
                ns[2 * d + half, :, cols] = stat[h : h + 1]
                ds[2 * d + half, :, cols] = stat[HEADS + h : HEADS + h + 1]
    acc[...] = jnp.zeros_like(acc) if is_first else acc_in[...]

    def tile(d, half, k, v, keep=None):
        i = 2 * d + half
        q = packs[d][pl.ds(pl.multiple_of(half * (2 * ROWS), ROWS), ROWS), :]
        g = packs[d][pl.ds(pl.multiple_of(half * (2 * ROWS) + ROWS, ROWS), ROWS), :]
        scores = dot(k, q, NT)
        probs = jnp.exp2(scores * (SCALE * LOG2E) - ns[i])
        if keep is not None:
            probs = jnp.where(keep, probs, 0.0)
        dprobs = dot(v, g, NT)
        dscores = (probs * (dprobs - ds[i]) * SCALE).astype(BF16)
        probs_low = probs.astype(BF16)
        dv = jnp.dot(probs_low, g, preferred_element_type=F32)
        dk = jnp.dot(dscores, q, preferred_element_type=F32)
        acc[i] += dot(k, dscores, TN)
        return dk, dv

    chunk = 4 if n_k % 4 == 0 else 3

    def first(c, carry):
        keys = pl.ds(pl.multiple_of(c * (chunk * HALF), chunk * HALF), chunk * HALF)
        k, v = ks[0, keys, :], vs[0, keys, :]
        dk = dv = 0.0
        for d in range(NY):
            dk_part, dv_part = tile(d, 1, k, v)
            dk, dv = dk + dk_part, dv + dv_part
        dks[0, keys, :] = dk
        dvs[0, keys, :] = dv
        dks[1, keys, :] = jnp.zeros_like(dk)
        dvs[1, keys, :] = jnp.zeros_like(dv)
        return carry

    lax.fori_loop(0, n_k // chunk, first, 0)

    def second(e, d):
        half = jnp.where(rk[e] < rq[d], 0, 1)
        keys = pl.ds(pl.multiple_of(e * HALF, HALF), HALF)
        dk, dv = tile(d, half, ks[half, keys, :], vs[half, keys, :])
        dks[half, keys, :] += dk
        dvs[half, keys, :] += dv

    def second_all(e, carry):
        for d in range(NY):
            second(e, d)
        return carry

    has_own = near[-1] == 0
    own_e = n_k - NX
    lax.fori_loop(0, own_e if has_own else n_k, second_all, 0)
    if has_own:
        second_all(own_e + 1, 0)
        for d in range(1, NY):
            second(own_e, d)
        keys = slice(own_e * HALF, (own_e + 1) * HALF)
        key_at = lax.broadcasted_iota(jnp.int32, (HALF, ROWS), 0)
        row_at = lax.broadcasted_iota(jnp.int32, (HALF, ROWS), 1) & (HALF - 1)
        keep = row_at >= key_at
        for half in range(2):
            dk, dv = tile(0, half, ks[half, keys, :], vs[half, keys, :], keep)
            dks[half, keys, :] += dk
            dvs[half, keys, :] += dv
    if is_last:
        for d in range(NY):
            for half in range(2):
                rows = slice(half * HALF, (half + 1) * HALF)
                for h in range(HEADS):
                    cols = slice(h * HEAD, (h + 1) * HEAD)
                    block = acc[2 * d + half, :, cols].T
                    dq_refs[d][rows, cols] = block if d == 0 else block.astype(BF16)
    for i, r in enumerate(near):
        for s in range(NX):
            for half in range(2):
                rows = slice(half * HALF, (half + 1) * HALF)
                e = NX * i + s
                keys = slice(e * HALF, (e + 1) * HALF)
                dk, dv = dks[half, keys, :], dvs[half, keys, :]
                out = dkv_refs[i].at[s]
                out[rows, :HEAD] = dk.astype(out.dtype)
                out[rows, HEAD:] = dv.astype(out.dtype)


def stage(near, me, pairing, packs, blocks, acc, is_last):
    m = len(near)
    pairs = NY * NX * m
    smem = pl.BlockSpec(memory_space=pltpu.SMEM)
    vmem = pl.BlockSpec(memory_space=pltpu.VMEM)
    sums = jax.ShapeDtypeStruct((2 * NY, HEAD, ROWS), F32)
    outs = [jax.ShapeDtypeStruct((NX, 2 * HALF, 2 * HEAD), F32 if r in OPEN else BF16) for r in near]
    if is_last:
        outs += [jax.ShapeDtypeStruct((2 * HALF, ROWS), F32 if d == 0 else BF16) for d in range(NY)]
    else:
        outs += [sums]
    first = [] if acc is None else [acc]

    def kernel(*refs):
        stage_kernel(near, acc is None, is_last, *refs)

    scratch = [pltpu.VMEM(sums.shape, F32)] if is_last else []
    return pl.pallas_call(
        kernel,
        out_shape=tuple(outs),
        in_specs=[smem, smem] + [vmem] * (NY + m + len(first)),
        out_specs=(vmem,) * len(outs),
        scratch_shapes=scratch
        + [
            pltpu.VMEM((2 * NY, 1, ROWS), F32),
            pltpu.VMEM((2 * NY, 1, ROWS), F32),
            pltpu.VMEM((2, NX * m * HALF, HEAD), BF16),
            pltpu.VMEM((2, NX * m * HALF, HEAD), BF16),
            pltpu.VMEM((2, NX * m * HALF, HEAD), F32),
            pltpu.VMEM((2, NX * m * HALF, HEAD), F32),
            pltpu.SMEM((NX * m,), jnp.int32),
        ],
        compiler_params=pltpu.CompilerParams(vmem_limit_bytes=32 * 1024 * 1024),
        cost_estimate=pl.CostEstimate(
            flops=pairs * 2 * 5 * 2 * HALF * HALF * ROWS * 2,
            bytes_accessed=4 * 1024 * 1024,
            transcendentals=pairs * 2 * HALF * ROWS,
        ),
    )(me, pairing, *packs, *blocks, *first)


def index_of(y, z, x):
    return (y * NZ + z) * NX + x


def shift(dy, dz, flip):
    return [
        (index_of((y + dy) % NY, (z + dz) % NZ, x ^ flip), index_of(y, z, x))
        for y in range(NY)
        for z in range(NZ)
        for x in range(NX)
    ]


def fetch(array, dy=0, dz=0, flip=0):
    return lax.ppermute(array, "ctx", shift(dy % NY, dz % NZ, flip))


def body(queries, key_head, value_head, attn_out, out_grads, log_norms, pairing):
    me = jnp.full((1,), lax.axis_index("ctx"), jnp.int32)
    pack, kv = pack_inputs(queries, out_grads, attn_out, log_norms, key_head, value_head)
    packs = {0: pack, 1: fetch(pack, dy=1), 3: fetch(pack, dy=-1)}
    packs[2] = fetch(packs[1], dy=1)
    blocks = {0: jnp.stack([kv, fetch(kv, flip=1)])}
    for r in (1, 2, 3):
        blocks[r] = fetch(blocks[r - 1], dz=1)
        blocks[NZ - r] = fetch(blocks[(NZ - r + 1) % NZ], dz=-1)
    blocks[4] = fetch(blocks[3], dz=1)

    acc = None
    up = down = None
    for at, near in enumerate(STAGES):
        is_last = at == len(STAGES) - 1
        outs = stage(near, me, pairing, [packs[d] for d in range(NY)], [blocks[r] for r in near], acc, is_last)
        acc = outs[2]
        if at == 0:
            up, down = outs[0], outs[1]
        elif not is_last:
            up = (outs[0] + up.astype(F32)).astype(BF16)
            down = (outs[1] + down.astype(F32)).astype(BF16)
        else:
            up = (outs[0] + up.astype(F32)).astype(BF16)
            dkv = outs[1] + down.astype(F32)
        up = fetch(up, dz=-1)
        if not is_last:
            down = fetch(down, dz=1)
    dq = acc
    for d in range(1, NY):
        dq = dq + fetch(outs[2 + d], dy=-d).astype(F32)
    dkv = dkv + up.astype(F32)
    dkv = dkv[0] + fetch(dkv[1].astype(BF16), flip=1).astype(F32)
    return dq, dkv[:, :HEAD], dkv[:, HEAD:]


def solution(mesh):
    rows = P(("dp", "ctx"), None)
    in_specs = (rows,) * 5 + (P(None, ("dp", "ctx")), P("dp"))
    return jax.shard_map(
        body, mesh=mesh, in_specs=in_specs, out_specs=(rows,) * 3, check_vma=False
    )
```

```python
import math

import jax
import jax.numpy as jnp
from jax import lax
from jax.experimental import pallas as pl
from jax.experimental.pallas import tpu as pltpu
from jax.sharding import PartitionSpec as P

F32 = jnp.float32
BF16 = jnp.bfloat16
HEAD = 128
HEADS = 4
HALF = 128
ROWS = HEADS * HALF
NY, NZ, NX = 4, 8, 2
SCALE = 1.0 / math.sqrt(HEAD)
LOG2E = math.log2(math.e)
NT = (((1,), (1,)), ((), ()))
TN = (((0,), (0,)), ((), ()))
PACK = 2 * 2 * ROWS
STATS = 48


def dot(a, b, dims):
    return lax.dot_general(a, b, dims, preferred_element_type=F32)


def pack_kernel(q_in, g_in, o_in, n_in, k_in, v_in, pack, kv, q_ref, g_ref, o_ref, n_ref, k_ref, v_ref, sems):
    pairs = [(k_in, k_ref), (v_in, v_ref), (q_in, q_ref), (g_in, g_ref), (o_in, o_ref), (n_in, n_ref)]
    copies = [pltpu.make_async_copy(s, t, sems.at[i]) for i, (s, t) in enumerate(pairs)]
    for copy in copies:
        copy.start()
    for copy in copies:
        copy.wait()
    for half in range(2):
        rows = slice(half * HALF, (half + 1) * HALF)
        kv[half, 0] = k_ref[rows, :]
        kv[half, 1] = v_ref[rows, :]
    terms = []
    for half in range(2):
        rows = slice(half * HALF, (half + 1) * HALF)
        deltas = []
        for h in range(HEADS):
            cols = slice(h * HEAD, (h + 1) * HEAD)
            q, g = q_ref[rows, cols], g_ref[rows, cols]
            at = half * 2 * ROWS + h * HALF
            pack[at : at + HALF, :] = q
            pack[at + ROWS : at + ROWS + HALF, :] = g
            product = o_ref[rows, cols].astype(F32) * g.astype(F32)
            deltas.append(jnp.sum(product.T, axis=0, keepdims=True))
        rest = jnp.concatenate([n_ref[:, rows] * LOG2E] + deltas, axis=0)
        for _ in range(3):
            term = rest.astype(BF16).astype(F32)
            rest = rest - term
            terms.append(term)
    pack[PACK:, :] = jnp.concatenate(terms, axis=0).astype(BF16)


def pack_inputs(queries, out_grads, attn_out, log_norms, key_head, value_head):
    vmem = pl.BlockSpec(memory_space=pltpu.VMEM)
    arrays = (queries, out_grads, attn_out, log_norms, key_head, value_head)
    return pl.pallas_call(
        pack_kernel,
        out_shape=(
            jax.ShapeDtypeStruct((PACK + STATS, HEAD), BF16),
            jax.ShapeDtypeStruct((2, 2, HALF, HEAD), BF16),
        ),
        in_specs=[pl.BlockSpec(memory_space=pl.ANY)] * 6,
        out_specs=(vmem,) * 2,
        scratch_shapes=[pltpu.VMEM(array.shape, array.dtype) for array in arrays]
        + [pltpu.SemaphoreType.DMA((6,))],
        compiler_params=pltpu.CompilerParams(vmem_limit_bytes=56 * 1024 * 1024),
    )(*arrays)


def stage_kernel(near, slots, more, held, seen, final, *refs):
    m = len(near)
    n_k = NX * m
    every = slots + more
    refs = list(refs)
    take = lambda n: [refs.pop(0) for _ in range(n)]
    me_ref, pairing = take(2)
    packs = dict(zip(every, take(len(every))))
    blocks = take(m)
    sums_in = take(m) if held else None
    acc_in = dict(zip(seen, take(len(seen))))
    dkv_refs = take(m)
    out_refs = dict(zip(every, take(len(every))))
    ns, ds, ks, vs, dks, dvs, dss, own_dss = take(8)

    me = me_ref[0]
    x, z, y = me & 1, (me >> 1) & (NZ - 1), me >> 4
    rq = {d: pairing[index_of((y + d) & (NY - 1), z, x)] for d in every}
    rk = []
    for i, r in enumerate(near):
        for s in range(NX):
            e = NX * i + s
            rk.append(pairing[index_of(y, (z + r) & (NZ - 1), x ^ s)])
            for half in range(2):
                rows = slice(half * HALF, (half + 1) * HALF)
                keys = slice(e * HALF, (e + 1) * HALF)
                ks[half, keys, :] = blocks[i][s, half, 0]
                vs[half, keys, :] = blocks[i][s, half, 1]
                if held:
                    dks[half, keys, :] = sums_in[i][s, rows, :HEAD]
                    dvs[half, keys, :] = sums_in[i][s, rows, HEAD:]
    if not held:
        dks[...] = jnp.zeros_like(dks)
        dvs[...] = jnp.zeros_like(dvs)
    for d in every:
        terms = packs[d][PACK:, :].astype(F32)
        for half in range(2):
            t = terms[24 * half : 24 * half + 24]
            stat = (t[0:8] + t[8:16]) + t[16:24]
            for h in range(HEADS):
                cols = slice(h * HALF, (h + 1) * HALF)
                ns[2 * d + half, :, cols] = stat[h : h + 1]
                ds[2 * d + half, :, cols] = stat[HEADS + h : HEADS + h + 1]

    def tile(d, half, k, v, keep=None):
        i = 2 * d + half
        q = packs[d][pl.ds(pl.multiple_of(half * (2 * ROWS), ROWS), ROWS), :]
        g = packs[d][pl.ds(pl.multiple_of(half * (2 * ROWS) + ROWS, ROWS), ROWS), :]
        scores = dot(k, q, NT)
        probs = jnp.exp2(scores * (SCALE * LOG2E) - ns[i])
        if keep is not None:
            probs = jnp.where(keep, probs, 0.0)
        dprobs = dot(v, g, NT)
        dscores = (probs * (dprobs - ds[i]) * SCALE).astype(BF16)
        probs_low = probs.astype(BF16)
        dv = jnp.dot(probs_low, g, preferred_element_type=F32)
        dk = jnp.dot(dscores, q, preferred_element_type=F32)
        return dk, dv, dscores

    def span(d):
        return n_k if d in slots else NX

    def block(e):
        return slice(e * HALF, (e + 1) * HALF)

    for d in every:
        keys = slice(0, span(d) * HALF)
        dk, dv, dscores = tile(d, 1, ks[0, keys, :], vs[0, keys, :])
        dks[0, keys, :] += dk
        dvs[0, keys, :] += dv
        dss[d, 0, keys, :] = dscores
    for e in range(n_k):
        keys = block(e)
        sums = [[0.0, 0.0], [0.0, 0.0]]
        for d in every:
            if e >= span(d):
                continue
            if d == 0 and near[e // NX] == 0 and e % NX == 0:
                key_at = lax.broadcasted_iota(jnp.int32, (HALF, ROWS), 0)
                row_at = lax.broadcasted_iota(jnp.int32, (HALF, ROWS), 1) & (HALF - 1)
                keep = row_at >= key_at
                for half in range(2):
                    dk, dv, dscores = tile(0, half, ks[half, keys, :], vs[half, keys, :], keep)
                    sums[half][0] += dk
                    sums[half][1] += dv
                    if half:
                        own_dss[...] = dscores
                    else:
                        dss[0, 1, keys, :] = dscores
                continue
            low = rk[e] < rq[d]
            half = jnp.where(low, 0, 1)
            dk, dv, dscores = tile(d, half, ks[half, keys, :], vs[half, keys, :])
            dss[d, 1, keys, :] = dscores
            for j, part in enumerate((dk, dv)):
                sums[0][j] += jnp.where(low, part, 0.0)
                sums[1][j] += jnp.where(low, 0.0, part)
        for half in range(2):
            dks[half, keys, :] += sums[half][0]
            dvs[half, keys, :] += sums[half][1]
    for d in every:
        keys = slice(0, span(d) * HALF)
        lower, upper = [], []
        for e in range(span(d)):
            k_low, k_high = ks[0, block(e), :], ks[1, block(e), :]
            none = jnp.zeros_like(k_low)
            if d == 0 and near[e // NX] == 0 and e % NX == 0:
                lower.append(k_low)
                upper.append(none)
            else:
                low = rk[e] < rq[d]
                lower.append(jnp.where(low, k_low, none))
                upper.append(jnp.where(low, none, k_high))
        dq = [
            dot(jnp.concatenate(lower, axis=0), dss[d, 1, keys, :], TN),
            dot(ks[0, keys, :], dss[d, 0, keys, :], TN)
            + dot(jnp.concatenate(upper, axis=0), dss[d, 1, keys, :], TN),
        ]
        if d == 0 and near[-1] == 0:
            dq[1] += dot(ks[1, block(n_k - NX), :], own_dss[...], TN)
        for half in range(2):
            total = dq[half] + acc_in[d][half] if d in seen else dq[half]
            if d not in final:
                out_refs[d][half] = total
                continue
            rows = slice(half * HALF, (half + 1) * HALF)
            for h in range(HEADS):
                cols = slice(h * HEAD, (h + 1) * HEAD)
                out_refs[d][rows, cols] = total[:, cols].T.astype(out_refs[d].dtype)
    for i in range(m):
        for s in range(NX):
            for half in range(2):
                rows = slice(half * HALF, (half + 1) * HALF)
                e = NX * i + s
                keys = slice(e * HALF, (e + 1) * HALF)
                out = dkv_refs[i].at[s]
                out[rows, :HEAD] = dks[half, keys, :].astype(out.dtype)
                out[rows, HEAD:] = dvs[half, keys, :].astype(out.dtype)


def stage(state, near, slots, more=(), final=(), narrow=False):
    m = len(near)
    every = slots + more
    pairs = NX * (len(slots) * m + len(more))
    held = near[-1] in state["dkv"]
    seen = tuple(d for d in every if d in state["dq"])
    smem = pl.BlockSpec(memory_space=pltpu.SMEM)
    vmem = pl.BlockSpec(memory_space=pltpu.VMEM)
    operands = [state["packs"][d] for d in every] + [state["blocks"][r] for r in near]
    if held:
        operands += [state["dkv"][r] for r in near]
    operands += [state["dq"][d] for d in seen]
    outs = [jax.ShapeDtypeStruct((NX, 2 * HALF, 2 * HEAD), BF16 if narrow else F32)] * m
    for d in every:
        if d in final:
            outs.append(jax.ShapeDtypeStruct((2 * HALF, ROWS), BF16 if d else F32))
        else:
            outs.append(jax.ShapeDtypeStruct((2, HEAD, ROWS), F32))

    def kernel(*refs):
        stage_kernel(near, slots, more, held, seen, final, *refs)

    results = pl.pallas_call(
        kernel,
        out_shape=tuple(outs),
        in_specs=[smem, smem] + [vmem] * len(operands),
        out_specs=(vmem,) * len(outs),
        scratch_shapes=[
            pltpu.VMEM((2 * NY, 1, ROWS), F32),
            pltpu.VMEM((2 * NY, 1, ROWS), F32),
            pltpu.VMEM((2, NX * m * HALF, HEAD), BF16),
            pltpu.VMEM((2, NX * m * HALF, HEAD), BF16),
            pltpu.VMEM((2, NX * m * HALF, HEAD), F32),
            pltpu.VMEM((2, NX * m * HALF, HEAD), F32),
            pltpu.VMEM((NY, 2, NX * m * HALF, ROWS), BF16),
            pltpu.VMEM((HALF, ROWS), BF16),
        ],
        compiler_params=pltpu.CompilerParams(vmem_limit_bytes=32 * 1024 * 1024),
        cost_estimate=pl.CostEstimate(
            flops=pairs * 2 * 5 * 2 * HALF * HALF * ROWS * 2,
            bytes_accessed=4 * 1024 * 1024,
            transcendentals=pairs * 2 * HALF * ROWS,
        ),
    )(state["me"], state["pairing"], *operands)
    state["dkv"].update(zip(near, results))
    state["dq"].update(zip(every, results[m:]))


def index_of(y, z, x):
    return (y * NZ + z) * NX + x


def shift(dy, dz, flip):
    return [
        (index_of((y + dy) % NY, (z + dz) % NZ, x ^ flip), index_of(y, z, x))
        for y in range(NY)
        for z in range(NZ)
        for x in range(NX)
    ]


def fetch(array, dy=0, dz=0, flip=0):
    return lax.ppermute(array, "ctx", shift(dy % NY, dz % NZ, flip))


def body(queries, key_head, value_head, attn_out, out_grads, log_norms, pairing):
    me = jnp.full((1,), lax.axis_index("ctx"), jnp.int32)
    pack, kv = pack_inputs(queries, out_grads, attn_out, log_norms, key_head, value_head)
    packs = {0: pack, 1: fetch(pack, dy=1), 3: fetch(pack, dy=-1)}
    packs[2] = fetch(packs[1], dy=1)
    blocks = {0: jnp.stack([kv, fetch(kv, flip=1)])}
    blocks[1], blocks[7] = fetch(blocks[0], dz=1), fetch(blocks[0], dz=-1)
    state = {"me": me, "pairing": pairing, "packs": packs, "blocks": blocks, "dkv": {}, "dq": {}}
    dkv, dq = state["dkv"], state["dq"]

    stage(state, (0,), (0,))
    blocks[1], blocks[7], dkv[0] = lax.optimization_barrier((blocks[1], blocks[7], dkv[0]))
    for r in (2, 3):
        blocks[r] = fetch(blocks[r - 1], dz=1)
        blocks[NZ - r] = fetch(blocks[NZ - r + 1], dz=-1)
    blocks[4] = fetch(blocks[3], dz=1)
    stage(state, (1, 7), (0,))
    stage(state, (2, 6), (0,))
    stage(state, (3, 5), (0,))
    far = (1, 2, 3)
    stage(state, (5,), far, narrow=True)
    stage(state, (4,), far + (0,), final=(0,), narrow=True)
    up, down = fetch(dkv[4], dz=-1), fetch(dkv[5], dz=1)
    for near in ((3, 6), (2, 7)):
        stage(state, near, far)
        up = fetch((dkv[near[0]] + up.astype(F32)).astype(BF16), dz=-1)
        down = fetch((dkv[near[1]] + down.astype(F32)).astype(BF16), dz=1)
    stage(state, (1, 0), far, final=far)
    up = fetch((dkv[1] + up.astype(F32)).astype(BF16), dz=-1)
    query_grad = dq[0]
    for d in far:
        query_grad = query_grad + fetch(dq[d], dy=-d).astype(F32)
    whole = dkv[0] + down.astype(F32) + up.astype(F32)
    whole = whole[0] + fetch(whole[1].astype(BF16), flip=1).astype(F32)
    return query_grad, whole[:, :HEAD], whole[:, HEAD:]


def solution(mesh):
    rows = P(("dp", "ctx"), None)
    in_specs = (rows,) * 5 + (P(None, ("dp", "ctx")), P("dp"))
    return jax.shard_map(
        body, mesh=mesh, in_specs=in_specs, out_specs=(rows,) * 3, check_vma=False
    )
```

```python
import math

import jax
import jax.numpy as jnp
from jax import lax
from jax.experimental import pallas as pl
from jax.experimental.pallas import tpu as pltpu
from jax.sharding import PartitionSpec as P

F32 = jnp.float32
BF16 = jnp.bfloat16
HEAD = 128
HEADS = 4
HALF = 128
ROWS = HEADS * HALF
NY, NZ, NX = 4, 8, 2
SCALE = 1.0 / math.sqrt(HEAD)
LOG2E = math.log2(math.e)
NT = (((1,), (1,)), ((), ()))
TN = (((0,), (0,)), ((), ()))
PACK = 2 * 2 * ROWS
STATS = 48


def dot(a, b, dims):
    return lax.dot_general(a, b, dims, preferred_element_type=F32)


def pack_kernel(q_in, g_in, o_in, n_in, pack, q_ref, g_ref, o_ref, n_ref, sems):
    pairs = [(q_in, q_ref), (g_in, g_ref), (o_in, o_ref), (n_in, n_ref)]
    copies = [pltpu.make_async_copy(s, t, sems.at[i]) for i, (s, t) in enumerate(pairs)]
    for copy in copies:
        copy.start()
    for copy in copies:
        copy.wait()
    terms = []
    for half in range(2):
        rows = slice(half * HALF, (half + 1) * HALF)
        deltas = []
        for h in range(HEADS):
            cols = slice(h * HEAD, (h + 1) * HEAD)
            q, g = q_ref[rows, cols], g_ref[rows, cols]
            at = half * 2 * ROWS + h * HALF
            pack[at : at + HALF, :] = q
            pack[at + ROWS : at + ROWS + HALF, :] = g
            product = o_ref[rows, cols].astype(F32) * g.astype(F32)
            deltas.append(jnp.sum(product.T, axis=0, keepdims=True))
        rest = jnp.concatenate([n_ref[:, rows] * LOG2E] + deltas, axis=0)
        for _ in range(3):
            term = rest.astype(BF16).astype(F32)
            rest = rest - term
            terms.append(term)
    pack[PACK:, :] = jnp.concatenate(terms, axis=0).astype(BF16)


def pack_inputs(queries, out_grads, attn_out, log_norms):
    vmem = pl.BlockSpec(memory_space=pltpu.VMEM)
    arrays = (queries, out_grads, attn_out, log_norms)
    return pl.pallas_call(
        pack_kernel,
        out_shape=jax.ShapeDtypeStruct((PACK + STATS, HEAD), BF16),
        in_specs=[pl.BlockSpec(memory_space=pl.ANY)] * len(arrays),
        out_specs=vmem,
        scratch_shapes=[pltpu.VMEM(array.shape, array.dtype) for array in arrays]
        + [pltpu.SemaphoreType.DMA((len(arrays),))],
        compiler_params=pltpu.CompilerParams(vmem_limit_bytes=56 * 1024 * 1024),
    )(*arrays)


def stage_kernel(near, slots, more, held, seen, final, *refs):
    m = len(near)
    n_k = NX * m
    every = slots + more
    refs = list(refs)
    take = lambda n: [refs.pop(0) for _ in range(n)]
    me_ref, pairing = take(2)
    packs = dict(zip(every, take(len(every))))
    blocks = take(m)
    sums_in = take(m) if held else None
    acc_in = dict(zip(seen, take(len(seen))))
    dkv_refs = take(m)
    out_refs = dict(zip(every, take(len(every))))
    ns, ds, ks, vs, dks, dvs, dss, own_dss = take(8)

    me = me_ref[0]
    x, z, y = me & 1, (me >> 1) & (NZ - 1), me >> 4
    rq = {d: pairing[index_of((y + d) & (NY - 1), z, x)] for d in every}
    rk = []
    for i, r in enumerate(near):
        for s in range(NX):
            e = NX * i + s
            rk.append(pairing[index_of(y, (z + r) & (NZ - 1), x ^ s)])
            for half in range(2):
                rows = slice(half * HALF, (half + 1) * HALF)
                keys = slice(e * HALF, (e + 1) * HALF)
                ks[half, keys, :] = blocks[i][s, 0, rows, :]
                vs[half, keys, :] = blocks[i][s, 1, rows, :]
                if held:
                    dks[half, keys, :] = sums_in[i][s, rows, :HEAD]
                    dvs[half, keys, :] = sums_in[i][s, rows, HEAD:]
    if not held:
        dks[...] = jnp.zeros_like(dks)
        dvs[...] = jnp.zeros_like(dvs)
    for d in every:
        terms = packs[d][PACK:, :].astype(F32)
        for half in range(2):
            t = terms[24 * half : 24 * half + 24]
            stat = (t[0:8] + t[8:16]) + t[16:24]
            for h in range(HEADS):
                cols = slice(h * HALF, (h + 1) * HALF)
                ns[2 * d + half, :, cols] = stat[h : h + 1]
                ds[2 * d + half, :, cols] = stat[HEADS + h : HEADS + h + 1]

    def tile(d, half, k, v, keep=None):
        i = 2 * d + half
        q = packs[d][pl.ds(pl.multiple_of(half * (2 * ROWS), ROWS), ROWS), :]
        g = packs[d][pl.ds(pl.multiple_of(half * (2 * ROWS) + ROWS, ROWS), ROWS), :]
        scores = dot(k, q, NT)
        probs = jnp.exp2(scores * (SCALE * LOG2E) - ns[i])
        if keep is not None:
            probs = jnp.where(keep, probs, 0.0)
        dprobs = dot(v, g, NT)
        dscores = (probs * (dprobs - ds[i]) * SCALE).astype(BF16)
        probs_low = probs.astype(BF16)
        dv = jnp.dot(probs_low, g, preferred_element_type=F32)
        dk = jnp.dot(dscores, q, preferred_element_type=F32)
        return dk, dv, dscores

    def span(d):
        return n_k if d in slots else NX

    def block(e):
        return slice(e * HALF, (e + 1) * HALF)

    for d in every:
        keys = slice(0, span(d) * HALF)
        dk, dv, dscores = tile(d, 1, ks[0, keys, :], vs[0, keys, :])
        dks[0, keys, :] += dk
        dvs[0, keys, :] += dv
        dss[d, 0, keys, :] = dscores
    for e in range(n_k):
        keys = block(e)
        sums = [[0.0, 0.0], [0.0, 0.0]]
        for d in every:
            if e >= span(d):
                continue
            if d == 0 and near[e // NX] == 0 and e % NX == 0:
                key_at = lax.broadcasted_iota(jnp.int32, (HALF, ROWS), 0)
                row_at = lax.broadcasted_iota(jnp.int32, (HALF, ROWS), 1) & (HALF - 1)
                keep = row_at >= key_at
                for half in range(2):
                    dk, dv, dscores = tile(0, half, ks[half, keys, :], vs[half, keys, :], keep)
                    sums[half][0] += dk
                    sums[half][1] += dv
                    if half:
                        own_dss[...] = dscores
                    else:
                        dss[0, 1, keys, :] = dscores
                continue
            low = rk[e] < rq[d]
            half = jnp.where(low, 0, 1)
            dk, dv, dscores = tile(d, half, ks[half, keys, :], vs[half, keys, :])
            dss[d, 1, keys, :] = dscores
            for j, part in enumerate((dk, dv)):
                sums[0][j] += jnp.where(low, part, 0.0)
                sums[1][j] += jnp.where(low, 0.0, part)
        for half in range(2):
            dks[half, keys, :] += sums[half][0]
            dvs[half, keys, :] += sums[half][1]
    for d in every:
        keys = slice(0, span(d) * HALF)
        lower, upper = [], []
        for e in range(span(d)):
            k_low, k_high = ks[0, block(e), :], ks[1, block(e), :]
            none = jnp.zeros_like(k_low)
            if d == 0 and near[e // NX] == 0 and e % NX == 0:
                lower.append(k_low)
                upper.append(none)
            else:
                low = rk[e] < rq[d]
                lower.append(jnp.where(low, k_low, none))
                upper.append(jnp.where(low, none, k_high))
        dq = [
            dot(jnp.concatenate(lower, axis=0), dss[d, 1, keys, :], TN),
            dot(ks[0, keys, :], dss[d, 0, keys, :], TN)
            + dot(jnp.concatenate(upper, axis=0), dss[d, 1, keys, :], TN),
        ]
        if d == 0 and near[-1] == 0:
            dq[1] += dot(ks[1, block(n_k - NX), :], own_dss[...], TN)
        for half in range(2):
            total = dq[half] + acc_in[d][half] if d in seen else dq[half]
            if d not in final:
                out_refs[d][half] = total
                continue
            rows = slice(half * HALF, (half + 1) * HALF)
            for h in range(HEADS):
                cols = slice(h * HEAD, (h + 1) * HEAD)
                out_refs[d][rows, cols] = total[:, cols].T.astype(out_refs[d].dtype)
    for i in range(m):
        for s in range(NX):
            for half in range(2):
                rows = slice(half * HALF, (half + 1) * HALF)
                e = NX * i + s
                keys = slice(e * HALF, (e + 1) * HALF)
                out = dkv_refs[i].at[s]
                out[rows, :HEAD] = dks[half, keys, :].astype(out.dtype)
                out[rows, HEAD:] = dvs[half, keys, :].astype(out.dtype)


def stage(state, near, slots, more=(), final=(), narrow=False):
    m = len(near)
    every = slots + more
    pairs = NX * (len(slots) * m + len(more))
    held = near[-1] in state["dkv"]
    seen = tuple(d for d in every if d in state["dq"])
    smem = pl.BlockSpec(memory_space=pltpu.SMEM)
    vmem = pl.BlockSpec(memory_space=pltpu.VMEM)
    operands = [state["packs"][d] for d in every] + [state["blocks"][r] for r in near]
    if held:
        operands += [state["dkv"][r] for r in near]
    operands += [state["dq"][d] for d in seen]
    outs = [jax.ShapeDtypeStruct((NX, 2 * HALF, 2 * HEAD), BF16 if narrow else F32)] * m
    for d in every:
        if d in final:
            outs.append(jax.ShapeDtypeStruct((2 * HALF, ROWS), BF16 if d else F32))
        else:
            outs.append(jax.ShapeDtypeStruct((2, HEAD, ROWS), F32))

    def kernel(*refs):
        stage_kernel(near, slots, more, held, seen, final, *refs)

    results = pl.pallas_call(
        kernel,
        out_shape=tuple(outs),
        in_specs=[smem, smem] + [vmem] * len(operands),
        out_specs=(vmem,) * len(outs),
        scratch_shapes=[
            pltpu.VMEM((2 * NY, 1, ROWS), F32),
            pltpu.VMEM((2 * NY, 1, ROWS), F32),
            pltpu.VMEM((2, NX * m * HALF, HEAD), BF16),
            pltpu.VMEM((2, NX * m * HALF, HEAD), BF16),
            pltpu.VMEM((2, NX * m * HALF, HEAD), F32),
            pltpu.VMEM((2, NX * m * HALF, HEAD), F32),
            pltpu.VMEM((NY, 2, NX * m * HALF, ROWS), BF16),
            pltpu.VMEM((HALF, ROWS), BF16),
        ],
        compiler_params=pltpu.CompilerParams(vmem_limit_bytes=32 * 1024 * 1024),
        cost_estimate=pl.CostEstimate(
            flops=pairs * 2 * 5 * 2 * HALF * HALF * ROWS * 2,
            bytes_accessed=4 * 1024 * 1024,
            transcendentals=pairs * 2 * HALF * ROWS,
        ),
    )(state["me"], state["pairing"], *operands)
    state["dkv"].update(zip(near, results))
    state["dq"].update(zip(every, results[m:]))


def index_of(y, z, x):
    return (y * NZ + z) * NX + x


def shift(dy, dz, flip):
    return [
        (index_of((y + dy) % NY, (z + dz) % NZ, x ^ flip), index_of(y, z, x))
        for y in range(NY)
        for z in range(NZ)
        for x in range(NX)
    ]


def fetch(array, dy=0, dz=0, flip=0):
    return lax.ppermute(array, "ctx", shift(dy % NY, dz % NZ, flip))


def body(queries, key_head, value_head, attn_out, out_grads, log_norms, pairing):
    me = jnp.full((1,), lax.axis_index("ctx"), jnp.int32)
    pair = [key_head, value_head]
    pair += [fetch(array, flip=1) for array in pair]
    pack = pack_inputs(queries, out_grads, attn_out, log_norms)
    packs = {0: pack, 1: fetch(pack, dy=1), 3: fetch(pack, dy=-1)}
    packs[2] = fetch(packs[1], dy=1)
    blocks = {0: jnp.stack(pair).reshape(NX, 2, 2 * HALF, HEAD)}
    blocks[1], blocks[7] = fetch(blocks[0], dz=1), fetch(blocks[0], dz=-1)
    state = {"me": me, "pairing": pairing, "packs": packs, "blocks": blocks, "dkv": {}, "dq": {}}
    dkv, dq = state["dkv"], state["dq"]

    stage(state, (0,), (0,))
    blocks[1], blocks[7], dkv[0] = lax.optimization_barrier((blocks[1], blocks[7], dkv[0]))
    for r in (2, 3):
        blocks[r] = fetch(blocks[r - 1], dz=1)
        blocks[NZ - r] = fetch(blocks[NZ - r + 1], dz=-1)
    blocks[4] = fetch(blocks[3], dz=1)
    stage(state, (1, 7), (0,))
    stage(state, (2, 6), (0,))
    stage(state, (3, 5), (0,))
    far = (1, 2, 3)
    stage(state, (5,), far, narrow=True)
    stage(state, (4,), far + (0,), final=(0,), narrow=True)
    up, down = fetch(dkv[4], dz=-1), fetch(dkv[5], dz=1)
    for near in ((3, 6), (2, 7)):
        stage(state, near, far)
        up = fetch((dkv[near[0]] + up.astype(F32)).astype(BF16), dz=-1)
        down = fetch((dkv[near[1]] + down.astype(F32)).astype(BF16), dz=1)
    stage(state, (1, 0), far, final=far)
    up = fetch((dkv[1] + up.astype(F32)).astype(BF16), dz=-1)
    query_grad = dq[0]
    for d in far:
        query_grad = query_grad + fetch(dq[d], dy=-d).astype(F32)
    whole = dkv[0] + down.astype(F32) + up.astype(F32)
    whole = whole[0] + fetch(whole[1].astype(BF16), flip=1).astype(F32)
    return query_grad, whole[:, :HEAD], whole[:, HEAD:]


def solution(mesh):
    rows = P(("dp", "ctx"), None)
    in_specs = (rows,) * 5 + (P(None, ("dp", "ctx")), P("dp"))
    return jax.shard_map(
        body, mesh=mesh, in_specs=in_specs, out_specs=(rows,) * 3, check_vma=False
    )
```
